32 devices in a mesh: pipe: 2 (over core), dp: 2 (over y), seq: 8 (over z, x).
Axes of the slice: x: 2, y: 2, z: 4, core: 2. Of those that a mesh axis runs over, the one named last changes fastest.
Arguments:
- section_feeds: bfloat16 [2, 3, 2, 1024, 640], P('pipe', None, 'dp', 'seq'), may hold values from -6 to 6
- positions: int32 [3, 2, 1024], P(None, 'dp', 'seq'), may hold values from 0 to 1023, as said below
- w_qkv: bfloat16 [2, 640, 1536], P('pipe', None, ('dp', 'seq')), may hold values from -0.25 to 0.25
- w_out: bfloat16 [2, 1024, 640], P('pipe', ('dp', 'seq')), may hold values from -0.1875 to 0.1875
- w_gate_up: bfloat16 [2, 640, 4096], P('pipe', None, ('dp', 'seq')), may hold values from -0.25 to 0.25
- w_down: bfloat16 [2, 2048, 640], P('pipe', ('dp', 'seq')), may hold values from -0.125 to 0.125
- gains: bfloat16 [2, 3072], P('pipe', ('dp', 'seq')), may hold values from 0.5 to 1.5
Outputs:
- section_ends: bfloat16 [2, 3, 2, 1024, 640], P('pipe', None, 'dp', 'seq')
- grad_qkv: float32 [2, 640, 1536], P('pipe', None, ('dp', 'seq'))
- grad_out: float32 [2, 1024, 640], P('pipe', ('dp', 'seq'))
- grad_gate_up: float32 [2, 640, 4096], P('pipe', None, ('dp', 'seq'))
- grad_down: float32 [2, 2048, 640], P('pipe', ('dp', 'seq'))
- grad_gains: float32 [2, 3072], P('pipe', ('dp', 'seq'))
The draws below stay inside these ranges and needn't reach their ends.
Inputs may be any that keep to these rules, and one draw needn't show every extreme that they name: `positions`: positions count from 0 at each document's start and rise by one within it. In each micro-batch one sequence, drawn from the seed, is a single document; the other holds up to four.
All inputs are finite; a program needn't handle non-finite values.
Results may differ from the reference program's by a relative error of at most 0.033.
Values may be sent and summed in bfloat16 or wider, within the bound.
A program may use at most 256 MiB of HBM per device.

```python
import jax
import jax.numpy as jnp
from jax import lax

D = 640
HEADS = 4
HEAD_DIM = 256
FF = 2048
MB = 3
WINDOW = 512
LEN = 1024
BATCH = 2
GAINS = 3072
QKV = 1536


def draw_positions(key, part):
    key = jax.random.fold_in(key, 7)
    whole_key, cut_key = jax.random.split(key)
    chosen = jax.random.randint(whole_key, (MB, 1), 0, BATCH)
    cuts = jax.random.randint(cut_key, (MB, BATCH, 3), 1, LEN)
    index_row = jnp.arange(LEN, dtype=jnp.int32)
    begun = jnp.where(cuts[..., None] <= index_row, cuts[..., None], 0)
    starts = jnp.max(begun, axis=2)
    single = jnp.arange(BATCH, dtype=jnp.int32)[None, :] == chosen
    starts = jnp.where(single[..., None], 0, starts)
    return (index_row[None, None, :] - starts).astype(jnp.int32)


def shard_levels(stream_key, shape, pieces, low, high):
    factor_of, own = 1.0, jax.random.fold_in(stream_key, 6)
    for axis_at, shards_of in pieces:
        draws = jnp.exp(jax.random.uniform(jax.random.fold_in(own, axis_at), (shards_of,), jnp.float32, low / len(pieces), high / len(pieces)))
        factor_of = factor_of * jnp.repeat(draws, shape[axis_at] // shards_of).reshape([-1 if axis == axis_at else 1 for axis in range(len(shape))])
    return factor_of


def scatter_about(stream_key, shape, deviation, most, cuts=(), held_as=jnp.bfloat16):
    gain = shard_levels(stream_key, shape, cuts, -0.22, 0.18) if cuts else 1.0
    values = jax.random.normal(stream_key, shape, jnp.float32) * deviation * gain
    return jnp.minimum(jnp.maximum(values, -most), most).astype(held_as)


def setup_inputs(seed: int = 0) -> dict:
    key_list = jax.random.split(jax.random.key(seed), 8)
    return {
        "section_feeds": scatter_about(key_list[0], (2, MB, BATCH, LEN, D), 1.0, 6.0, ((0, 2), (2, 2), (3, 8))),
        "positions": draw_positions(jax.random.fold_in(key_list[7], 71), 0),
        "w_qkv": scatter_about(key_list[2], (2, D, QKV), D ** -0.5, 0.25, ((0, 2), (2, 16))),
        "w_out": scatter_about(key_list[3], (2, HEADS * HEAD_DIM, D), (HEADS * HEAD_DIM) ** -0.5, 0.1875, ((0, 2), (1, 16))),
        "w_gate_up": scatter_about(key_list[4], (2, D, 2 * FF), D ** -0.5, 0.25, ((0, 2), (2, 16))),
        "w_down": scatter_about(key_list[5], (2, FF, D), FF ** -0.5, 0.125, ((0, 2), (1, 16))),
        "gains": jnp.clip(1.0 + 0.1 * jax.random.normal(key_list[6], (2, GAINS), jnp.float32), 0.5, 1.5).astype(jnp.bfloat16),
    }


@jax.custom_vjp
def low(v):
    return lax.optimization_barrier(v.astype(jnp.bfloat16)).astype(jnp.float32)

@jax.custom_vjp
def low_back(v):
    return v

def low_keep(v):
    return (low(v), None)

def low_pass(kept, grad):
    return (grad,)

def back_keep(v):
    return (v, None)

def back_low(kept, grad):
    return (low(grad),)
low.defvjp(low_keep, low_pass)
low_back.defvjp(back_keep, back_low)
epsilon = 1e-06
negative = -1e+30
highest = lax.Precision.HIGHEST

def product(left, right):
    return jnp.dot(left, right, precision=highest)

def rms_scale(values, scale_gain):
    return values * lax.rsqrt(lax.optimization_barrier(jnp.mean(values * values, axis=-1, keepdims=True)) + epsilon) * scale_gain

def rotate(values, position, rope_base):
    half_size = values.shape[-1] // 2
    frequency = rope_base ** (-2.0 * jnp.arange(half_size, dtype=jnp.float32) / values.shape[-1])
    angles = position.astype(jnp.float32)[:, None] * frequency[None, :]
    cosine = jnp.cos(angles)
    sine_part = jnp.sin(angles)
    front_half = values[..., :half_size]
    back_half = values[..., half_size:]
    return jnp.concatenate([front_half * cosine - back_half * sine_part, back_half * cosine + front_half * sine_part], axis=-1)

def attention(queries, key_rows, value_rows, position, window):
    block_rows = min(512, LEN)
    score_scale = HEAD_DIM ** (-0.5)
    key_index = jnp.arange(LEN, dtype=jnp.int32)

    def one_block(block_index):
        begin_row = (block_index * block_rows).astype(jnp.int32)
        query_block = lax.dynamic_slice_in_dim(queries, begin_row, block_rows, 1)
        query_place = lax.dynamic_slice_in_dim(position, begin_row, block_rows, 0)
        query_index = begin_row + jnp.arange(block_rows, dtype=jnp.int32)
        scores = low_back(jnp.einsum('hqd,kd->hqk', query_block, key_rows, precision=highest) * score_scale)
        distance = query_index[:, None] - key_index[None, :]
        visible = (distance >= 0) & (distance <= query_place[:, None]) & (distance < window)
        scores = jnp.where(visible[None], scores, negative)
        top_score = lax.optimization_barrier(jnp.max(scores, axis=-1, keepdims=True))
        weights = jnp.exp(scores - top_score)
        probability = low(weights / lax.optimization_barrier(jnp.sum(weights, axis=-1, keepdims=True)))
        return jnp.einsum('hqk,kd->hqd', probability, value_rows, precision=highest)
    blocks = lax.map(jax.checkpoint(one_block), jnp.arange(LEN // block_rows, dtype=jnp.int32))
    return blocks.transpose(1, 0, 2, 3).reshape(HEADS, LEN, HEAD_DIM)

def decoder_layer(inputs, position, parameters, rope_base, window):
    w_qkv, w_out, w_gate_up, w_down, gains = parameters
    width = HEADS * HEAD_DIM
    normed = low(rms_scale(inputs, gains[:D]))
    projected = low_back(product(normed, w_qkv))
    queries = projected[:, :width].reshape(LEN, HEADS, HEAD_DIM).transpose(1, 0, 2)
    queries = low(rotate(rms_scale(queries, gains[4 * D:4 * D + HEAD_DIM]), position, rope_base))
    key_rows = low(rotate(rms_scale(projected[:, width:width + HEAD_DIM], gains[4 * D + HEAD_DIM:]), position, rope_base))
    value_rows = low(projected[:, width + HEAD_DIM:])
    attended = attention(queries, key_rows, value_rows, position, window)
    attended = low_back(low(attended.transpose(1, 0, 2).reshape(LEN, width)))
    branch = low_back(product(attended, w_out))
    hidden = inputs + rms_scale(branch, gains[D:2 * D])
    normed_ffw = low(rms_scale(hidden, gains[2 * D:3 * D]))
    gate_up = low_back(product(normed_ffw, w_gate_up))
    activated = low(jax.nn.gelu(gate_up[:, :FF], approximate=True) * gate_up[:, FF:])
    branch_ffw = low_back(product(activated, w_down))
    return hidden + rms_scale(branch_ffw, gains[3 * D:4 * D])

def two_layers(sequence, position, parameters):
    lower = tuple((matrix[0] for matrix in parameters))
    upper = tuple((matrix[1] for matrix in parameters))
    middle = decoder_layer(sequence, position, lower, 1000000.0, LEN)
    middle = low_back(low(middle))
    return decoder_layer(middle, position, upper, 10000.0, WINDOW)

def reference(section_feeds, positions, w_qkv, w_out, w_gate_up, w_down, gains):
    parameters = tuple((matrix.astype(jnp.float32) for matrix in (w_qkv, w_out, w_gate_up, w_down, gains)))
    flat_inputs = section_feeds[0].astype(jnp.float32).reshape(MB * BATCH, LEN, D)
    flat_cotangent = section_feeds[1].astype(jnp.float32).reshape(MB * BATCH, LEN, D)
    flat_places = positions.reshape(MB * BATCH, LEN)

    def per_sequence(totals, item):
        sequence, position, cotangent_rows = item
        outputs, pullback = jax.vjp(lambda seq_in, params_in: two_layers(seq_in, position, params_in), sequence, parameters)
        grad_input, grad_params = pullback(cotangent_rows)
        totals = tuple((running + fresh for running, fresh in zip(totals, grad_params)))
        return (totals, (outputs, grad_input))
    zeros_start = tuple((jnp.zeros(matrix.shape, jnp.float32) for matrix in parameters))
    totals, (outputs, grad_inputs) = lax.scan(per_sequence, zeros_start, (flat_inputs, flat_places, flat_cotangent))
    section_ends = jnp.stack([grad_inputs.reshape(MB, BATCH, LEN, D), outputs.reshape(MB, BATCH, LEN, D)]).astype(jnp.bfloat16)
    return (section_ends, totals[0], totals[1], totals[2], totals[3], totals[4])
```

```python
import jax
import jax.numpy as jnp
from jax import lax
from jax.sharding import PartitionSpec as P

D = 640
HEADS = 4
HEAD_DIM = 256
FF = 2048
WINDOW = 512


epsilon = 1e-06
negative = -1e30


def rms_scale(values, scale_gain):
    return (
        values * lax.rsqrt(jnp.mean(values * values, axis=-1, keepdims=True) + epsilon) * scale_gain
    )


def geglu(gate_up):
    return jax.nn.gelu(gate_up[:, :FF], approximate=True) * gate_up[:, FF:]


def contract_rows(left, right):
    return lax.dot_general(
        left, right, (((0,), (0,)), ((), ())), preferred_element_type=jnp.float32
    )


def contract_cols(left, right):
    return lax.dot_general(
        left, right, (((1,), (1,)), ((), ())), preferred_element_type=jnp.float32
    )


def swapped(array):
    return lax.ppermute(array, "pipe", [(0, 1), (1, 0)])


def rotate(values, cosine, sine_part):
    half_size = values.shape[-1] // 2
    front_half = values[..., :half_size]
    back_half = values[..., half_size:]
    return jnp.concatenate(
        [front_half * cosine - back_half * sine_part, back_half * cosine + front_half * sine_part],
        axis=-1,
    )


def angle_tables(position, rope_base):
    half_size = HEAD_DIM // 2
    frequency = rope_base ** (-2.0 * jnp.arange(half_size, dtype=jnp.float32) / HEAD_DIM)
    angles = position.astype(jnp.float32)[..., None] * frequency
    return (jnp.cos(angles), jnp.sin(angles))


def stack_heads(rows, micro_count):
    return jnp.stack(
        [
            rows[:, h * HEAD_DIM : (h + 1) * HEAD_DIM].reshape(micro_count, -1, HEAD_DIM)
            for h in range(HEADS)
        ],
        axis=1,
    )


def side_by_side(stacked):
    return jnp.concatenate([stacked[:, h].reshape(-1, HEAD_DIM) for h in range(HEADS)], axis=1)


def split_heads(projected, query_gain, key_gain, tables):
    cosine, sine_part = tables
    micro_count = cosine.shape[0]
    width = HEADS * HEAD_DIM
    queries = stack_heads(projected[:, :width], micro_count)
    queries = rotate(rms_scale(queries, query_gain), cosine[:, None], sine_part[:, None])
    key_rows = projected[:, width : width + HEAD_DIM].reshape(micro_count, -1, HEAD_DIM)
    key_rows = rotate(rms_scale(key_rows, key_gain), cosine, sine_part)
    value_rows = projected[:, width + HEAD_DIM :].reshape(micro_count, -1, HEAD_DIM)
    return (queries, key_rows, value_rows)


def by_micro(equation, left, right):
    return jnp.einsum(equation, left, right, preferred_element_type=jnp.float32)


def visibility(query_index, position, key_index, window):
    distance = query_index[None, :, None] - key_index[None, None, :]
    visible = (distance >= 0) & (distance <= position[:, :, None])
    if window is not None:
        visible = visible & (distance < window)
    return visible


def gather_keys(packed):
    everyone = lax.all_gather(packed, ("pipe", "seq"), axis=0)
    micro_count = packed.shape[0]
    return everyone.transpose(1, 0, 2, 3).reshape(micro_count, -1, 2 * HEAD_DIM)


def scatter_keys(grad_keys, row_count):
    micro_count = grad_keys.shape[0]
    pieces = grad_keys.reshape(micro_count, -1, row_count, 2 * HEAD_DIM).transpose(1, 0, 2, 3)
    pieces = pieces.reshape(-1, 2 * HEAD_DIM)
    own = lax.psum_scatter(pieces, ("pipe", "seq"), scatter_dimension=0, tiled=True)
    return own.reshape(micro_count, row_count, 2 * HEAD_DIM).astype(jnp.float32)


def forward_layer(inputs, weights, tables, visible):
    w_qkv, w_out, w_gate_up, w_down, gains = weights
    micro_count, row_count = tables[0].shape[:2]
    normed = rms_scale(inputs, gains[:D]).astype(jnp.bfloat16)
    projected = contract_cols(normed, w_qkv)
    queries, key_rows, value_rows = split_heads(
        projected, gains[4 * D : 4 * D + HEAD_DIM], gains[4 * D + HEAD_DIM :], tables
    )
    packed = jnp.concatenate([key_rows, value_rows], axis=-1).astype(jnp.bfloat16)
    keys = gather_keys(packed)
    queries = queries.astype(jnp.bfloat16).reshape(micro_count, HEADS * row_count, HEAD_DIM)
    scores = by_micro("mqd,mkd->mqk", queries, keys[..., :HEAD_DIM]) * HEAD_DIM ** (-0.5)
    scores = jnp.where(visible, scores, negative)
    top_score = jnp.max(scores, axis=-1, keepdims=True)
    unscaled = jnp.where(visible, jnp.exp(scores - top_score), 0.0)
    denominator = jnp.sum(unscaled, axis=-1, keepdims=True)
    probability = unscaled / denominator
    gathered = by_micro("mqk,mkd->mqd", probability.astype(jnp.bfloat16), keys[..., HEAD_DIM:])
    attended = side_by_side(
        gathered.reshape(micro_count, HEADS, row_count, HEAD_DIM).astype(jnp.bfloat16)
    )
    branch = jnp.dot(attended, w_out, preferred_element_type=jnp.float32)
    hidden = inputs + rms_scale(branch, gains[D : 2 * D])
    normed_ffw = rms_scale(hidden, gains[2 * D : 3 * D]).astype(jnp.bfloat16)
    gate_up = contract_cols(normed_ffw, w_gate_up)
    activated = geglu(gate_up).astype(jnp.bfloat16)
    branch_ffw = jnp.dot(activated, w_down, preferred_element_type=jnp.float32)
    output = hidden + rms_scale(branch_ffw, gains[3 * D : 4 * D])
    kept = (
        inputs, normed, projected, queries, keys, probability, gathered, attended,
        branch, hidden, normed_ffw, gate_up, activated, branch_ffw,
    )
    return (output, kept)


def backward_layer(incoming, kept, weights, tables):
    w_qkv, w_out, w_gate_up, w_down, gains = weights
    (
        inputs, normed, projected, queries, keys, probability, gathered, attended,
        branch, hidden, normed_ffw, gate_up, activated, branch_ffw,
    ) = kept
    micro_count, row_count = tables[0].shape[:2]
    score_scale = HEAD_DIM ** (-0.5)
    unused, pullback = jax.vjp(rms_scale, branch_ffw, gains[3 * D : 4 * D])
    grad_branch_ffw, gain_post_ffw = pullback(incoming)
    grad_branch_ffw = grad_branch_ffw.astype(jnp.bfloat16)
    grad_w_down = contract_rows(activated, grad_branch_ffw)
    grad_activated = contract_cols(grad_branch_ffw, w_down)
    unused, pullback = jax.vjp(geglu, gate_up)
    grad_gate_up = pullback(grad_activated)[0].astype(jnp.bfloat16)
    grad_w_gate_up = contract_rows(grad_gate_up, normed_ffw)
    grad_normed_ffw = jnp.dot(grad_gate_up, w_gate_up, preferred_element_type=jnp.float32)
    unused, pullback = jax.vjp(rms_scale, hidden, gains[2 * D : 3 * D])
    grad_hidden, gain_pre_ffw = pullback(grad_normed_ffw)
    grad_hidden = grad_hidden + incoming
    unused, pullback = jax.vjp(rms_scale, branch, gains[D : 2 * D])
    grad_branch, gain_post_attn = pullback(grad_hidden)
    grad_branch = grad_branch.astype(jnp.bfloat16)
    grad_w_out = contract_rows(attended, grad_branch)
    grad_attended = contract_cols(grad_branch, w_out).astype(jnp.bfloat16)
    grad_rows = stack_heads(grad_attended, micro_count)
    grad_rows = grad_rows.reshape(micro_count, HEADS * row_count, HEAD_DIM)
    row_delta = jnp.sum(grad_rows.astype(jnp.float32) * gathered, axis=-1, keepdims=True)
    grad_probability = by_micro("mqd,mkd->mqk", grad_rows, keys[..., HEAD_DIM:])
    grad_scores = (probability * (grad_probability - row_delta)).astype(jnp.bfloat16)
    key_part = by_micro("mqk,mqd->mkd", grad_scores, queries) * score_scale
    value_part = by_micro("mqk,mqd->mkd", probability.astype(jnp.bfloat16), grad_rows)
    grad_keys = jnp.concatenate([key_part, value_part], axis=-1).astype(jnp.bfloat16)
    grad_keys = scatter_keys(grad_keys, row_count)
    grad_queries = by_micro("mqk,mkd->mqd", grad_scores, keys[..., :HEAD_DIM]) * score_scale
    grad_queries = grad_queries.reshape(micro_count, HEADS, row_count, HEAD_DIM)
    unused, pullback = jax.vjp(
        lambda projected, query_gain, key_gain: split_heads(
            projected, query_gain, key_gain, tables
        ),
        projected,
        gains[4 * D : 4 * D + HEAD_DIM],
        gains[4 * D + HEAD_DIM :],
    )
    grad_projected, gain_query, gain_key = pullback(
        (grad_queries, grad_keys[..., :HEAD_DIM], grad_keys[..., HEAD_DIM:])
    )
    grad_projected = grad_projected.astype(jnp.bfloat16)
    grad_w_qkv = contract_rows(grad_projected, normed)
    grad_normed = jnp.dot(grad_projected, w_qkv, preferred_element_type=jnp.float32)
    unused, pullback = jax.vjp(rms_scale, inputs, gains[:D])
    grad_inputs, gain_pre_attn = pullback(grad_normed)
    grad_inputs = grad_inputs + grad_hidden
    gain_grads = jnp.concatenate(
        [gain_pre_attn, gain_post_attn, gain_pre_ffw, gain_post_ffw, gain_query, gain_key]
    )
    return (grad_inputs, (grad_w_qkv, grad_w_out, grad_w_gate_up, grad_w_down, gain_grads))


def both_layers(shard, leading):
    own = lax.all_gather(shard, ("dp", "seq"), axis=0)
    other = swapped(own)
    return (own, other)


def rows_of(pair, layer, leading, begin, count):
    own, other = pair
    first = leading if layer == 0 else jnp.logical_not(leading)
    piece = jnp.where(first, own[:, begin : begin + count], other[:, begin : begin + count])
    return piece.reshape(-1, piece.shape[-1])


def reduce_group(grads, leading, owners):
    pieces = jnp.concatenate(
        [g.astype(jnp.bfloat16).reshape(owners, -1, D) for g in grads], axis=1
    )
    half = pieces.shape[1] // 2
    front, back = pieces[:, :half], pieces[:, half:]
    received = swapped(jnp.where(leading, back, front))
    summed = jnp.where(leading, front, back) + received
    summed = summed.reshape(owners * half, D)
    return lax.psum_scatter(summed, ("dp", "seq"), scatter_dimension=0, tiled=True)


def hand_over(lower, upper, leading):
    sent = jnp.where(leading, upper, lower)
    mine = jnp.where(leading, lower, upper)
    received = swapped(sent)
    return (jnp.where(leading, mine, received), jnp.where(leading, received, mine))


GAIN_ROWS = 16


def on_device(section_feeds, positions, w_qkv, w_out, w_gate_up, w_down, gains):
    leading = lax.axis_index("pipe") == 0
    pipe_rank = lax.axis_index("pipe")
    seq_rank = lax.axis_index("seq")
    seq_size = lax.axis_size("seq")
    owners = lax.axis_size("dp") * seq_size
    qkv_rows, out_rows = w_qkv.shape[2], w_out.shape[1]
    gate_up_rows, down_rows = w_gate_up.shape[2], w_down.shape[1]
    gain_count = gains.shape[1]
    gain_block = jnp.pad(gains, ((0, GAIN_ROWS - 1), (0, D - gain_count)))
    early = jnp.concatenate([w_qkv[0].T, w_out[0], gain_block], axis=0)
    late = jnp.concatenate([w_gate_up[0].T, w_down[0]], axis=0)
    early = both_layers(early, leading)
    late = both_layers(late, leading)

    def layer_weights(layer):
        own_gains = rows_of(early, layer, leading, qkv_rows + out_rows, 1)
        return (
            rows_of(early, layer, leading, 0, qkv_rows),
            rows_of(early, layer, leading, qkv_rows, out_rows),
            rows_of(late, layer, leading, 0, gate_up_rows),
            rows_of(late, layer, leading, gate_up_rows, down_rows),
            own_gains[:, :gain_count].reshape(-1).astype(jnp.float32),
        )

    feeds = section_feeds[0, :, 0]
    micro_count, shard_rows = feeds.shape[:2]
    row_count = shard_rows // 2
    front, back = feeds[:, :row_count], feeds[:, row_count:]
    received = swapped(jnp.where(leading, back, front))
    first_in = jnp.where(leading, front, received).reshape(-1, D)
    last_grad = jnp.where(leading, received, back).reshape(-1, D)
    begin = pipe_rank * row_count
    position = lax.dynamic_slice_in_dim(positions[:, 0], begin, row_count, 1)
    local_rows = jnp.arange(row_count, dtype=jnp.int32)
    query_index = seq_rank * shard_rows + begin + local_rows
    key_index = (
        jnp.arange(2, dtype=jnp.int32)[:, None, None] * row_count
        + jnp.arange(seq_size, dtype=jnp.int32)[None, :, None] * shard_rows
        + local_rows[None, None, :]
    ).reshape(-1)
    query_index = jnp.tile(query_index, HEADS)
    query_place = jnp.tile(position, (1, HEADS))

    lower = layer_weights(0)
    upper = layer_weights(1)
    tables = (angle_tables(position, 1000000.0), angle_tables(position, 10000.0))
    visible = (
        visibility(query_index, query_place, key_index, None),
        visibility(query_index, query_place, key_index, WINDOW),
    )
    middle, kept_lower = forward_layer(first_in.astype(jnp.float32), lower, tables[0], visible[0])
    middle = middle.astype(jnp.bfloat16).astype(jnp.float32)
    output, kept_upper = forward_layer(middle, upper, tables[1], visible[1])
    output = output.astype(jnp.bfloat16)

    def reduce_layer(grads):
        grad_qkv, grad_out, grad_gate_up, grad_down, gain_grads = grads
        gain_rows = jnp.pad(
            gain_grads.reshape(owners, 1, gain_count),
            ((0, 0), (0, GAIN_ROWS - 1), (0, D - gain_count)),
        )
        return (
            reduce_group((grad_gate_up, grad_down), leading, owners),
            reduce_group((grad_qkv, grad_out, gain_rows), leading, owners),
        )

    grad_middle, grads = backward_layer(last_grad.astype(jnp.float32), kept_upper, upper, tables[1])
    upper_parts = reduce_layer(grads)
    grad_middle = grad_middle.astype(jnp.bfloat16).astype(jnp.float32)
    grad_input, grads = backward_layer(grad_middle, kept_lower, lower, tables[0])
    lower_parts = reduce_layer(grads)
    ends = hand_over(
        grad_input.astype(jnp.bfloat16).reshape(micro_count, row_count, D),
        output.reshape(micro_count, row_count, D),
        leading,
    )
    section_end = jnp.concatenate(ends, axis=1)
    late_grads = jnp.concatenate(hand_over(lower_parts[0], upper_parts[0], leading), axis=0)
    early_grads = jnp.concatenate(hand_over(lower_parts[1], upper_parts[1], leading), axis=0)
    late_grads = late_grads.astype(jnp.float32)
    early_grads = early_grads.astype(jnp.float32)
    return (
        section_end[None, :, None],
        early_grads[:qkv_rows].T[None],
        early_grads[qkv_rows : qkv_rows + out_rows][None],
        late_grads[:gate_up_rows].T[None],
        late_grads[gate_up_rows:][None],
        early_grads[qkv_rows + out_rows, :gain_count][None],
    )


def solution(mesh):
    in_specs = (
        P("pipe", None, "dp", "seq", None),
        P(None, "dp", "seq"),
        P("pipe", None, ("dp", "seq")),
        P("pipe", ("dp", "seq"), None),
        P("pipe", None, ("dp", "seq")),
        P("pipe", ("dp", "seq"), None),
        P("pipe", ("dp", "seq")),
    )
    out_specs = (
        P("pipe", None, "dp", "seq", None),
        P("pipe", None, ("dp", "seq")),
        P("pipe", ("dp", "seq"), None),
        P("pipe", None, ("dp", "seq")),
        P("pipe", ("dp", "seq"), None),
        P("pipe", ("dp", "seq")),
    )
    return jax.shard_map(
        on_device, mesh=mesh, in_specs=in_specs, out_specs=out_specs, check_vma=False
    )
```

```python
import jax
import jax.numpy as jnp
from jax import lax
from jax.sharding import PartitionSpec as P

D = 640
HEADS = 4
HEAD_DIM = 256
FF = 2048
WINDOW = 512


epsilon = 1e-06
negative = -1e30


def rms_scale(values, scale_gain):
    return (
        values * lax.rsqrt(jnp.mean(values * values, axis=-1, keepdims=True) + epsilon) * scale_gain
    )


def geglu(gate_up):
    return jax.nn.gelu(gate_up[:, :FF], approximate=True) * gate_up[:, FF:]


def contract_rows(left, right):
    return lax.dot_general(
        left, right, (((0,), (0,)), ((), ())), preferred_element_type=jnp.float32
    )


def contract_cols(left, right):
    return lax.dot_general(
        left, right, (((1,), (1,)), ((), ())), preferred_element_type=jnp.float32
    )


def swapped(array):
    return lax.ppermute(array, "pipe", [(0, 1), (1, 0)])


def rotate(values, cosine, sine_part):
    half_size = values.shape[-1] // 2
    front_half = values[..., :half_size]
    back_half = values[..., half_size:]
    return jnp.concatenate(
        [front_half * cosine - back_half * sine_part, back_half * cosine + front_half * sine_part],
        axis=-1,
    )


def angle_tables(position, rope_base):
    half_size = HEAD_DIM // 2
    frequency = rope_base ** (-2.0 * jnp.arange(half_size, dtype=jnp.float32) / HEAD_DIM)
    angles = position.astype(jnp.float32)[..., None] * frequency
    return (jnp.cos(angles), jnp.sin(angles))


def stack_heads(rows, micro_count):
    return jnp.stack(
        [
            rows[:, h * HEAD_DIM : (h + 1) * HEAD_DIM].reshape(micro_count, -1, HEAD_DIM)
            for h in range(HEADS)
        ],
        axis=1,
    )


def side_by_side(stacked):
    return jnp.concatenate([stacked[:, h].reshape(-1, HEAD_DIM) for h in range(HEADS)], axis=1)


def split_heads(projected, query_gain, key_gain, tables):
    cosine, sine_part = tables
    micro_count = cosine.shape[0]
    width = HEADS * HEAD_DIM
    queries = stack_heads(projected[:, :width], micro_count)
    queries = rotate(rms_scale(queries, query_gain), cosine[:, None], sine_part[:, None])
    key_rows = projected[:, width : width + HEAD_DIM].reshape(micro_count, -1, HEAD_DIM)
    key_rows = rotate(rms_scale(key_rows, key_gain), cosine, sine_part)
    value_rows = projected[:, width + HEAD_DIM :].reshape(micro_count, -1, HEAD_DIM)
    return (queries, key_rows, value_rows)


def by_micro(equation, left, right):
    return jnp.einsum(equation, left, right, preferred_element_type=jnp.float32)


def visibility(query_index, position, key_index, window):
    distance = query_index[None, :, None] - key_index[None, None, :]
    visible = (distance >= 0) & (distance <= position[:, :, None])
    if window is not None:
        visible = visible & (distance < window)
    return visible


def gather_keys(packed):
    everyone = lax.all_gather(packed, ("pipe", "seq"), axis=0)
    micro_count = packed.shape[0]
    return everyone.transpose(1, 0, 2, 3).reshape(micro_count, -1, 2 * HEAD_DIM)


def scatter_keys(grad_keys, row_count):
    micro_count = grad_keys.shape[0]
    pieces = grad_keys.reshape(micro_count, -1, row_count, 2 * HEAD_DIM).transpose(1, 0, 2, 3)
    pieces = pieces.reshape(-1, 2 * HEAD_DIM)
    own = lax.psum_scatter(pieces, ("pipe", "seq"), scatter_dimension=0, tiled=True)
    return own.reshape(micro_count, row_count, 2 * HEAD_DIM).astype(jnp.float32)


def forward_layer(inputs, weights, tables, visible):
    w_qkv, w_out, w_gate_up, w_down, gains = weights
    micro_count, row_count = tables[0].shape[:2]
    normed = rms_scale(inputs, gains[:D]).astype(jnp.bfloat16)
    projected = contract_cols(normed, w_qkv)
    queries, key_rows, value_rows = split_heads(
        projected, gains[4 * D : 4 * D + HEAD_DIM], gains[4 * D + HEAD_DIM :], tables
    )
    packed = jnp.concatenate([key_rows, value_rows], axis=-1).astype(jnp.bfloat16)
    keys = gather_keys(packed)
    queries = queries.astype(jnp.bfloat16).reshape(micro_count, HEADS * row_count, HEAD_DIM)
    scores = by_micro("mqd,mkd->mqk", queries, keys[..., :HEAD_DIM]) * HEAD_DIM ** (-0.5)
    scores = jnp.where(visible, scores, negative)
    top_score = jnp.max(scores, axis=-1, keepdims=True)
    unscaled = jnp.where(visible, jnp.exp(scores - top_score), 0.0)
    denominator = jnp.sum(unscaled, axis=-1, keepdims=True)
    probability = unscaled / denominator
    gathered = by_micro("mqk,mkd->mqd", probability.astype(jnp.bfloat16), keys[..., HEAD_DIM:])
    attended = side_by_side(
        gathered.reshape(micro_count, HEADS, row_count, HEAD_DIM).astype(jnp.bfloat16)
    )
    branch = jnp.dot(attended, w_out, preferred_element_type=jnp.float32)
    hidden = inputs + rms_scale(branch, gains[D : 2 * D])
    normed_ffw = rms_scale(hidden, gains[2 * D : 3 * D]).astype(jnp.bfloat16)
    gate_up = contract_cols(normed_ffw, w_gate_up)
    activated = geglu(gate_up).astype(jnp.bfloat16)
    branch_ffw = jnp.dot(activated, w_down, preferred_element_type=jnp.float32)
    output = hidden + rms_scale(branch_ffw, gains[3 * D : 4 * D])
    kept = (
        inputs, normed, projected, queries, keys, probability, gathered, attended,
        branch, hidden, normed_ffw, gate_up, activated, branch_ffw,
    )
    return (output, kept)


def backward_layer(incoming, kept, weights, tables, leading, pending):
    w_qkv, w_out, w_gate_up, w_down, gains = weights
    (
        inputs, normed, projected, queries, keys, probability, gathered, attended,
        branch, hidden, normed_ffw, gate_up, activated, branch_ffw,
    ) = kept
    micro_count, row_count = tables[0].shape[:2]
    owners = lax.axis_size("dp") * lax.axis_size("seq")
    score_scale = HEAD_DIM ** (-0.5)
    unused, pullback = jax.vjp(rms_scale, branch_ffw, gains[3 * D : 4 * D])
    grad_branch_ffw, gain_post_ffw = pullback(incoming)
    grad_branch_ffw = grad_branch_ffw.astype(jnp.bfloat16)
    grad_w_down = contract_rows(activated, grad_branch_ffw)
    grad_activated = contract_cols(grad_branch_ffw, w_down)
    unused, pullback = jax.vjp(geglu, gate_up)
    grad_gate_up = pullback(grad_activated)[0].astype(jnp.bfloat16)
    grad_w_gate_up = contract_rows(grad_gate_up, normed_ffw)
    grad_normed_ffw = jnp.dot(grad_gate_up, w_gate_up, preferred_element_type=jnp.float32)
    unused, pullback = jax.vjp(rms_scale, hidden, gains[2 * D : 3 * D])
    grad_hidden, gain_pre_ffw = pullback(grad_normed_ffw)
    grad_hidden = grad_hidden + incoming
    own_chains = start_group((grad_w_gate_up, grad_w_down), leading, owners)
    if pending:
        grad_hidden, pending = held_until(grad_hidden, advance(pending, 2))
    unused, pullback = jax.vjp(rms_scale, branch, gains[D : 2 * D])
    grad_branch, gain_post_attn = pullback(grad_hidden)
    grad_branch = grad_branch.astype(jnp.bfloat16)
    grad_w_out = contract_rows(attended, grad_branch)
    grad_attended = contract_cols(grad_branch, w_out).astype(jnp.bfloat16)
    grad_rows = stack_heads(grad_attended, micro_count)
    grad_rows = grad_rows.reshape(micro_count, HEADS * row_count, HEAD_DIM)
    row_delta = jnp.sum(grad_rows.astype(jnp.float32) * gathered, axis=-1, keepdims=True)
    grad_probability = by_micro("mqd,mkd->mqk", grad_rows, keys[..., HEAD_DIM:])
    grad_scores = (probability * (grad_probability - row_delta)).astype(jnp.bfloat16)
    key_part = by_micro("mqk,mqd->mkd", grad_scores, queries) * score_scale
    value_part = by_micro("mqk,mqd->mkd", probability.astype(jnp.bfloat16), grad_rows)
    grad_keys = jnp.concatenate([key_part, value_part], axis=-1).astype(jnp.bfloat16)
    grad_keys = scatter_keys(grad_keys, row_count)
    waiting = advance(own_chains, 2) + advance(pending, seq_bits() + 1)
    grad_keys, waiting = held_until(grad_keys, waiting)
    own_chains, pending = waiting[:2], waiting[2:]
    grad_queries = by_micro("mqk,mkd->mqd", grad_scores, keys[..., :HEAD_DIM]) * score_scale
    grad_queries = grad_queries.reshape(micro_count, HEADS, row_count, HEAD_DIM)
    unused, pullback = jax.vjp(
        lambda projected, query_gain, key_gain: split_heads(
            projected, query_gain, key_gain, tables
        ),
        projected,
        gains[4 * D : 4 * D + HEAD_DIM],
        gains[4 * D + HEAD_DIM :],
    )
    grad_projected, gain_query, gain_key = pullback(
        (grad_queries, grad_keys[..., :HEAD_DIM], grad_keys[..., HEAD_DIM:])
    )
    grad_projected = grad_projected.astype(jnp.bfloat16)
    grad_w_qkv = contract_rows(grad_projected, normed)
    grad_normed = jnp.dot(grad_projected, w_qkv, preferred_element_type=jnp.float32)
    unused, pullback = jax.vjp(rms_scale, inputs, gains[:D])
    grad_inputs, gain_pre_attn = pullback(grad_normed)
    grad_inputs = grad_inputs + grad_hidden
    gain_grads = jnp.concatenate(
        [gain_pre_attn, gain_post_attn, gain_pre_ffw, gain_post_ffw, gain_query, gain_key]
    )
    gain_rows = gain_grads.reshape(owners, 1, -1)
    gain_rows = jnp.pad(gain_rows, ((0, 0), (0, GAIN_ROWS - 1), (0, D - gain_rows.shape[-1])))
    last_chains = start_group((grad_w_qkv, grad_w_out, gain_rows), leading, owners)
    return (grad_inputs, own_chains + last_chains, pending)


def seq_bits():
    return lax.axis_size("seq").bit_length() - 1


def across(array, dim):
    if dim == 0:
        return lax.ppermute(array, "dp", [(0, 1), (1, 0)])
    step = 1 << (seq_bits() - dim)
    size = lax.axis_size("seq")
    return lax.ppermute(array, "seq", [(i, i ^ step) for i in range(size)])


def upper_side(dim):
    if dim == 0:
        return lax.axis_index("dp") == 1
    return ((lax.axis_index("seq") >> (seq_bits() - dim)) & 1) == 1


def halving_order(first):
    last = seq_bits()
    inner = list(range(last - 1, 0, -1))
    return ([last, 0] if first else [0, last]) + inner


def gathered_by_doubling(shard, first):
    piece = shard.reshape((1,) * (seq_bits() + 1) + shard.shape)
    for dim in halving_order(first)[::-1]:
        received = across(piece, dim)
        piece = jnp.where(
            upper_side(dim),
            jnp.concatenate([received, piece], axis=dim),
            jnp.concatenate([piece, received], axis=dim),
        )
    return piece.reshape((-1,) + shard.shape)


def advance(chains, count):
    moved = []
    for total, order in chains:
        for dim in order[:count]:
            low_half = lax.slice_in_dim(total, 0, 1, axis=dim)
            high_half = lax.slice_in_dim(total, 1, 2, axis=dim)
            high = upper_side(dim)
            received = across(jnp.where(high, low_half, high_half), dim)
            total = jnp.where(high, high_half, low_half) + received
        moved.append((total, order[count:]))
    return moved


def finish(chains):
    ends = [total for total, order in advance(chains, seq_bits() + 1)]
    return jnp.concatenate([total.reshape(total.shape[-2:]) for total in ends], axis=0)


def held_until(array, chains):
    tied = lax.optimization_barrier((array,) + tuple(total for total, order in chains))
    return (tied[0], [(total, chain[1]) for total, chain in zip(tied[1:], chains)])


def start_group(grads, leading, owners):
    pieces = jnp.concatenate(
        [g.astype(jnp.bfloat16).reshape(owners, -1, D) for g in grads], axis=1
    )
    half = pieces.shape[1] // 2
    front, back = pieces[:, :half], pieces[:, half:]
    received = swapped(jnp.where(leading, back, front))
    summed = jnp.where(leading, front, back) + received
    cut = -(-half // 32) * 16 if half > 32 else half // 2
    sizes = (2,) * (seq_bits() + 1)
    return [
        (piece.reshape(sizes + piece.shape[1:]), halving_order(first))
        for piece, first in ((summed[:, :cut], True), (summed[:, cut:], False))
    ]


def both_layers(shard):
    own = lax.all_gather(shard, ("dp", "seq"), axis=0)
    return (own, swapped(own))


def both_layers_by_doubling(shard):
    half = shard.shape[0] // 2
    chains = [gathered_by_doubling(shard[:half], True), gathered_by_doubling(shard[half:], False)]
    own = jnp.concatenate(chains, axis=1)
    other = jnp.concatenate([swapped(chain) for chain in chains], axis=1)
    return (own, other)


def rows_of(pair, layer, leading, begin, count):
    own, other = pair
    first = leading if layer == 0 else jnp.logical_not(leading)
    piece = jnp.where(first, own[:, begin : begin + count], other[:, begin : begin + count])
    return piece.reshape(-1, piece.shape[-1])


def hand_over(lower, upper, leading):
    sent = jnp.where(leading, upper, lower)
    mine = jnp.where(leading, lower, upper)
    received = swapped(sent)
    return (jnp.where(leading, mine, received), jnp.where(leading, received, mine))


GAIN_ROWS = 16


def on_device(section_feeds, positions, w_qkv, w_out, w_gate_up, w_down, gains):
    leading = lax.axis_index("pipe") == 0
    pipe_rank = lax.axis_index("pipe")
    seq_rank = lax.axis_index("seq")
    seq_size = lax.axis_size("seq")
    owners = lax.axis_size("dp") * seq_size
    qkv_rows, out_rows = w_qkv.shape[2], w_out.shape[1]
    gate_up_rows, down_rows = w_gate_up.shape[2], w_down.shape[1]
    gain_count = gains.shape[1]
    gain_block = jnp.pad(gains, ((0, GAIN_ROWS - 1), (0, D - gain_count)))
    early = jnp.concatenate([w_qkv[0].T, w_out[0], gain_block], axis=0)
    late = jnp.concatenate([w_gate_up[0].T, w_down[0]], axis=0)
    early = both_layers(early)
    late = both_layers_by_doubling(late)

    def layer_weights(layer):
        own_gains = rows_of(early, layer, leading, qkv_rows + out_rows, 1)
        return (
            rows_of(early, layer, leading, 0, qkv_rows),
            rows_of(early, layer, leading, qkv_rows, out_rows),
            rows_of(late, layer, leading, 0, gate_up_rows),
            rows_of(late, layer, leading, gate_up_rows, down_rows),
            own_gains[:, :gain_count].reshape(-1).astype(jnp.float32),
        )

    feeds = section_feeds[0, :, 0]
    micro_count, shard_rows = feeds.shape[:2]
    row_count = shard_rows // 2
    front, back = feeds[:, :row_count], feeds[:, row_count:]
    received = swapped(jnp.where(leading, back, front))
    first_in = jnp.where(leading, front, received).reshape(-1, D)
    last_grad = jnp.where(leading, received, back).reshape(-1, D)
    begin = pipe_rank * row_count
    position = lax.dynamic_slice_in_dim(positions[:, 0], begin, row_count, 1)
    local_rows = jnp.arange(row_count, dtype=jnp.int32)
    query_index = seq_rank * shard_rows + begin + local_rows
    key_index = (
        jnp.arange(2, dtype=jnp.int32)[:, None, None] * row_count
        + jnp.arange(seq_size, dtype=jnp.int32)[None, :, None] * shard_rows
        + local_rows[None, None, :]
    ).reshape(-1)
    query_index = jnp.tile(query_index, HEADS)
    query_place = jnp.tile(position, (1, HEADS))

    lower = layer_weights(0)
    upper = layer_weights(1)
    tables = (angle_tables(position, 1000000.0), angle_tables(position, 10000.0))
    visible = (
        visibility(query_index, query_place, key_index, None),
        visibility(query_index, query_place, key_index, WINDOW),
    )
    middle, kept_lower = forward_layer(first_in.astype(jnp.float32), lower, tables[0], visible[0])
    middle = middle.astype(jnp.bfloat16).astype(jnp.float32)
    output, kept_upper = forward_layer(middle, upper, tables[1], visible[1])
    output = output.astype(jnp.bfloat16)

    grad_middle, upper_chains, unused = backward_layer(
        last_grad.astype(jnp.float32), kept_upper, upper, tables[1], leading, []
    )
    grad_middle = grad_middle.astype(jnp.bfloat16).astype(jnp.float32)
    grad_input, lower_chains, upper_chains = backward_layer(
        grad_middle, kept_lower, lower, tables[0], leading, upper_chains
    )
    upper_parts = (finish(upper_chains[:2]), finish(upper_chains[2:]))
    lower_parts = (finish(lower_chains[:2]), finish(lower_chains[2:]))
    ends = hand_over(
        grad_input.astype(jnp.bfloat16).reshape(micro_count, row_count, D),
        output.reshape(micro_count, row_count, D),
        leading,
    )
    section_end = jnp.concatenate(ends, axis=1)
    late_grads = jnp.concatenate(hand_over(lower_parts[0], upper_parts[0], leading), axis=0)
    early_grads = jnp.concatenate(hand_over(lower_parts[1], upper_parts[1], leading), axis=0)
    late_grads = late_grads.astype(jnp.float32)
    early_grads = early_grads.astype(jnp.float32)
    return (
        section_end[None, :, None],
        early_grads[:qkv_rows].T[None],
        early_grads[qkv_rows : qkv_rows + out_rows][None],
        late_grads[:gate_up_rows].T[None],
        late_grads[gate_up_rows:][None],
        early_grads[qkv_rows + out_rows, :gain_count][None],
    )


def solution(mesh):
    in_specs = (
        P("pipe", None, "dp", "seq", None),
        P(None, "dp", "seq"),
        P("pipe", None, ("dp", "seq")),
        P("pipe", ("dp", "seq"), None),
        P("pipe", None, ("dp", "seq")),
        P("pipe", ("dp", "seq"), None),
        P("pipe", ("dp", "seq")),
    )
    out_specs = (
        P("pipe", None, "dp", "seq", None),
        P("pipe", None, ("dp", "seq")),
        P("pipe", ("dp", "seq"), None),
        P("pipe", None, ("dp", "seq")),
        P("pipe", ("dp", "seq"), None),
        P("pipe", ("dp", "seq")),
    )
    return jax.shard_map(
        on_device, mesh=mesh, in_specs=in_specs, out_specs=out_specs, check_vma=False
    )
```

```python
import jax
import jax.numpy as jnp
from jax import lax
from jax.sharding import PartitionSpec as P

D = 640
HEADS = 4
HEAD_DIM = 256
FF = 2048
WINDOW = 512


epsilon = 1e-06
negative = -1e30


def rms_scale(values, scale_gain):
    return (
        values * lax.rsqrt(jnp.mean(values * values, axis=-1, keepdims=True) + epsilon) * scale_gain
    )


def geglu(gate_up):
    return jax.nn.gelu(gate_up[:, :FF], approximate=True) * gate_up[:, FF:]


def contract_rows(left, right):
    return lax.dot_general(
        left, right, (((0,), (0,)), ((), ())), preferred_element_type=jnp.float32
    )


def contract_cols(left, right):
    return lax.dot_general(
        left, right, (((1,), (1,)), ((), ())), preferred_element_type=jnp.float32
    )


def swapped(array):
    return lax.ppermute(array, "pipe", [(0, 1), (1, 0)])


def rotate(values, cosine, sine_part):
    half_size = values.shape[-1] // 2
    front_half = values[..., :half_size]
    back_half = values[..., half_size:]
    return jnp.concatenate(
        [front_half * cosine - back_half * sine_part, back_half * cosine + front_half * sine_part],
        axis=-1,
    )


def angle_tables(position, rope_base):
    half_size = HEAD_DIM // 2
    frequency = rope_base ** (-2.0 * jnp.arange(half_size, dtype=jnp.float32) / HEAD_DIM)
    angles = position.astype(jnp.float32)[..., None] * frequency
    return (jnp.cos(angles), jnp.sin(angles))


def stack_heads(rows, micro_count):
    return jnp.stack(
        [
            rows[:, h * HEAD_DIM : (h + 1) * HEAD_DIM].reshape(micro_count, -1, HEAD_DIM)
            for h in range(HEADS)
        ],
        axis=1,
    )


def side_by_side(stacked):
    return jnp.concatenate([stacked[:, h].reshape(-1, HEAD_DIM) for h in range(HEADS)], axis=1)


def split_heads(projected, query_gain, key_gain, tables):
    cosine, sine_part = tables
    micro_count = cosine.shape[0]
    width = HEADS * HEAD_DIM
    queries = stack_heads(projected[:, :width], micro_count)
    queries = rotate(rms_scale(queries, query_gain), cosine[:, None], sine_part[:, None])
    key_rows = projected[:, width : width + HEAD_DIM].reshape(micro_count, -1, HEAD_DIM)
    key_rows = rotate(rms_scale(key_rows, key_gain), cosine, sine_part)
    value_rows = projected[:, width + HEAD_DIM :].reshape(micro_count, -1, HEAD_DIM)
    return (queries, key_rows, value_rows)


def by_micro(equation, left, right):
    return jnp.einsum(equation, left, right, preferred_element_type=jnp.float32)


def visibility(query_index, position, key_index, window):
    distance = query_index[None, :, None] - key_index[None, None, :]
    visible = (distance >= 0) & (distance <= position[:, :, None])
    if window is not None:
        visible = visible & (distance < window)
    return visible


def gather_keys(packed):
    everyone = lax.all_gather(packed, ("pipe", "seq"), axis=0)
    micro_count = packed.shape[0]
    return everyone.transpose(1, 0, 2, 3).reshape(micro_count, -1, 2 * HEAD_DIM)


def scatter_keys(grad_keys, row_count):
    micro_count = grad_keys.shape[0]
    pieces = grad_keys.reshape(micro_count, -1, row_count, 2 * HEAD_DIM).transpose(1, 0, 2, 3)
    pieces = pieces.reshape(-1, 2 * HEAD_DIM)
    own = lax.psum_scatter(pieces, ("pipe", "seq"), scatter_dimension=0, tiled=True)
    return own.reshape(micro_count, row_count, 2 * HEAD_DIM).astype(jnp.float32)


def forward_layer(inputs, first_weights, tables, visible, late_weights):
    w_qkv, w_out, gains = first_weights
    micro_count, row_count = tables[0].shape[:2]
    normed = rms_scale(inputs, gains[:D]).astype(jnp.bfloat16)
    projected = contract_cols(normed, w_qkv)
    queries, key_rows, value_rows = split_heads(
        projected, gains[4 * D : 4 * D + HEAD_DIM], gains[4 * D + HEAD_DIM :], tables
    )
    packed = jnp.concatenate([key_rows, value_rows], axis=-1).astype(jnp.bfloat16)
    packed, chains = late_weights.begin(packed)
    keys = gather_keys(packed)
    queries = queries.astype(jnp.bfloat16).reshape(micro_count, HEADS * row_count, HEAD_DIM)
    scores = by_micro("mqd,mkd->mqk", queries, keys[..., :HEAD_DIM]) * HEAD_DIM ** (-0.5)
    scores = jnp.where(visible, scores, negative)
    top_score = jnp.max(scores, axis=-1, keepdims=True)
    unscaled = jnp.where(visible, jnp.exp(scores - top_score), 0.0)
    denominator = jnp.sum(unscaled, axis=-1, keepdims=True)
    probability = unscaled / denominator
    gathered = by_micro("mqk,mkd->mqd", probability.astype(jnp.bfloat16), keys[..., HEAD_DIM:])
    attended = side_by_side(
        gathered.reshape(micro_count, HEADS, row_count, HEAD_DIM).astype(jnp.bfloat16)
    )
    attended, w_gate_up, w_down = late_weights.end(attended, chains)
    branch = jnp.dot(attended, w_out, preferred_element_type=jnp.float32)
    hidden = inputs + rms_scale(branch, gains[D : 2 * D])
    normed_ffw = rms_scale(hidden, gains[2 * D : 3 * D]).astype(jnp.bfloat16)
    gate_up = contract_cols(normed_ffw, w_gate_up)
    activated = geglu(gate_up).astype(jnp.bfloat16)
    branch_ffw = jnp.dot(activated, w_down, preferred_element_type=jnp.float32)
    output = hidden + rms_scale(branch_ffw, gains[3 * D : 4 * D])
    kept = (
        inputs, normed, projected, queries, keys, probability, gathered, attended,
        branch, hidden, normed_ffw, gate_up, activated, branch_ffw,
    )
    return (output, kept, (w_qkv, w_out, w_gate_up, w_down, gains))


def backward_layer(incoming, kept, weights, tables, leading, pending):
    w_qkv, w_out, w_gate_up, w_down, gains = weights
    (
        inputs, normed, projected, queries, keys, probability, gathered, attended,
        branch, hidden, normed_ffw, gate_up, activated, branch_ffw,
    ) = kept
    micro_count, row_count = tables[0].shape[:2]
    owners = lax.axis_size("dp") * lax.axis_size("seq")
    score_scale = HEAD_DIM ** (-0.5)
    unused, pullback = jax.vjp(rms_scale, branch_ffw, gains[3 * D : 4 * D])
    grad_branch_ffw, gain_post_ffw = pullback(incoming)
    grad_branch_ffw = grad_branch_ffw.astype(jnp.bfloat16)
    grad_w_down = contract_rows(activated, grad_branch_ffw)
    grad_activated = contract_cols(grad_branch_ffw, w_down)
    unused, pullback = jax.vjp(geglu, gate_up)
    grad_gate_up = pullback(grad_activated)[0].astype(jnp.bfloat16)
    grad_w_gate_up = contract_rows(grad_gate_up, normed_ffw)
    grad_normed_ffw = jnp.dot(grad_gate_up, w_gate_up, preferred_element_type=jnp.float32)
    unused, pullback = jax.vjp(rms_scale, hidden, gains[2 * D : 3 * D])
    grad_hidden, gain_pre_ffw = pullback(grad_normed_ffw)
    grad_hidden = grad_hidden + incoming
    if pending:
        grad_hidden, pending = held_until(grad_hidden, advance(pending, 2))
    unused, pullback = jax.vjp(rms_scale, branch, gains[D : 2 * D])
    grad_branch, gain_post_attn = pullback(grad_hidden)
    grad_branch = grad_branch.astype(jnp.bfloat16)
    grad_w_out = contract_rows(attended, grad_branch)
    own_chains = start_group((grad_w_gate_up, grad_w_down, grad_w_out), leading, owners)
    grad_attended = contract_cols(grad_branch, w_out).astype(jnp.bfloat16)
    grad_rows = stack_heads(grad_attended, micro_count)
    grad_rows = grad_rows.reshape(micro_count, HEADS * row_count, HEAD_DIM)
    row_delta = jnp.sum(grad_rows.astype(jnp.float32) * gathered, axis=-1, keepdims=True)
    grad_probability = by_micro("mqd,mkd->mqk", grad_rows, keys[..., HEAD_DIM:])
    grad_scores = (probability * (grad_probability - row_delta)).astype(jnp.bfloat16)
    key_part = by_micro("mqk,mqd->mkd", grad_scores, queries) * score_scale
    value_part = by_micro("mqk,mqd->mkd", probability.astype(jnp.bfloat16), grad_rows)
    grad_keys = jnp.concatenate([key_part, value_part], axis=-1).astype(jnp.bfloat16)
    grad_keys = scatter_keys(grad_keys, row_count)
    waiting = advance(own_chains, 2) + advance(pending, seq_bits() + 1)
    grad_keys, waiting = held_until(grad_keys, waiting)
    own_chains, pending = waiting[:2], waiting[2:]
    grad_queries = by_micro("mqk,mkd->mqd", grad_scores, keys[..., :HEAD_DIM]) * score_scale
    grad_queries = grad_queries.reshape(micro_count, HEADS, row_count, HEAD_DIM)
    unused, pullback = jax.vjp(
        lambda projected, query_gain, key_gain: split_heads(
            projected, query_gain, key_gain, tables
        ),
        projected,
        gains[4 * D : 4 * D + HEAD_DIM],
        gains[4 * D + HEAD_DIM :],
    )
    grad_projected, gain_query, gain_key = pullback(
        (grad_queries, grad_keys[..., :HEAD_DIM], grad_keys[..., HEAD_DIM:])
    )
    grad_projected = grad_projected.astype(jnp.bfloat16)
    grad_w_qkv = contract_rows(grad_projected, normed)
    grad_normed = jnp.dot(grad_projected, w_qkv, preferred_element_type=jnp.float32)
    unused, pullback = jax.vjp(rms_scale, inputs, gains[:D])
    grad_inputs, gain_pre_attn = pullback(grad_normed)
    grad_inputs = grad_inputs + grad_hidden
    gain_grads = jnp.concatenate(
        [gain_pre_attn, gain_post_attn, gain_pre_ffw, gain_post_ffw, gain_query, gain_key]
    )
    gain_rows = gain_grads.reshape(owners, 1, -1)
    gain_rows = jnp.pad(gain_rows, ((0, 0), (0, GAIN_ROWS - 1), (0, D - gain_rows.shape[-1])))
    last_chains = start_group((grad_w_qkv, gain_rows), leading, owners)
    return (grad_inputs, own_chains + last_chains, pending)


def seq_bits():
    return lax.axis_size("seq").bit_length() - 1


def across(array, dim):
    if dim == 0:
        return lax.ppermute(array, "dp", [(0, 1), (1, 0)])
    step = 1 << (seq_bits() - dim)
    size = lax.axis_size("seq")
    return lax.ppermute(array, "seq", [(i, i ^ step) for i in range(size)])


def upper_side(dim):
    if dim == 0:
        return lax.axis_index("dp") == 1
    return ((lax.axis_index("seq") >> (seq_bits() - dim)) & 1) == 1


def halving_order(first):
    last = seq_bits()
    inner = list(range(last - 1, 0, -1))
    return ([last, 0] if first else [0, last]) + inner


def start_doubling(shard):
    half = shard.shape[0] // 2
    ones = (1,) * (seq_bits() + 1)
    return [
        (piece.reshape(ones + piece.shape), halving_order(first)[::-1])
        for piece, first in ((shard[:half], True), (shard[half:], False))
    ]


def double(chains, count):
    moved = []
    for piece, order in chains:
        for dim in order[:count]:
            received = across(piece, dim)
            piece = jnp.where(
                upper_side(dim),
                jnp.concatenate([received, piece], axis=dim),
                jnp.concatenate([piece, received], axis=dim),
            )
        moved.append((piece, order[count:]))
    return moved


def doubled(chains):
    pieces = [piece for piece, order in double(chains, seq_bits() + 1)]
    pieces = [piece.reshape((-1,) + piece.shape[-2:]) for piece in pieces]
    own = jnp.concatenate(pieces, axis=1)
    other = jnp.concatenate([swapped(piece) for piece in pieces], axis=1)
    return (own, other)


def advance(chains, count):
    moved = []
    for total, order in chains:
        for dim in order[:count]:
            low_half = lax.slice_in_dim(total, 0, 1, axis=dim)
            high_half = lax.slice_in_dim(total, 1, 2, axis=dim)
            high = upper_side(dim)
            received = across(jnp.where(high, low_half, high_half), dim)
            total = jnp.where(high, high_half, low_half) + received
        moved.append((total, order[count:]))
    return moved


def finish(chains):
    ends = [total for total, order in advance(chains, seq_bits() + 1)]
    return jnp.concatenate([total.reshape(total.shape[-2:]) for total in ends], axis=0)


def held_until(array, chains):
    tied = lax.optimization_barrier((array,) + tuple(total for total, order in chains))
    return (tied[0], [(total, chain[1]) for total, chain in zip(tied[1:], chains)])


def start_group(grads, leading, owners):
    pieces = jnp.concatenate(
        [g.astype(jnp.bfloat16).reshape(owners, -1, D) for g in grads], axis=1
    )
    half = pieces.shape[1] // 2
    front, back = pieces[:, :half], pieces[:, half:]
    received = swapped(jnp.where(leading, back, front))
    summed = jnp.where(leading, front, back) + received
    cut = -(-half // 32) * 16 if half > 32 else half // 2
    sizes = (2,) * (seq_bits() + 1)
    return [
        (piece.reshape(sizes + piece.shape[1:]), halving_order(first))
        for piece, first in ((summed[:, :cut], True), (summed[:, cut:], False))
    ]


def start_group(grads, leading, owners):
    pieces = jnp.concatenate(
        [g.astype(jnp.bfloat16).reshape(owners, -1, D) for g in grads], axis=1
    )
    half = pieces.shape[1] // 2
    front, back = pieces[:, :half], pieces[:, half:]
    received = swapped(jnp.where(leading, back, front))
    summed = jnp.where(leading, front, back) + received
    cut = -(-half // 32) * 16 if half > 32 else half // 2
    sizes = (2,) * (seq_bits() + 1)
    return [
        (piece.reshape(sizes + piece.shape[1:]), halving_order(first))
        for piece, first in ((summed[:, :cut], True), (summed[:, cut:], False))
    ]


def both_layers(shard):
    own = lax.all_gather(shard, ("dp", "seq"), axis=0)
    return (own, swapped(own))


def both_layers_by_doubling(shard):
    half = shard.shape[0] // 2
    chains = [gathered_by_doubling(shard[:half], True), gathered_by_doubling(shard[half:], False)]
    own = jnp.concatenate(chains, axis=1)
    other = jnp.concatenate([swapped(chain) for chain in chains], axis=1)
    return (own, other)


def rows_of(pair, layer, leading, begin, count):
    own, other = pair
    first = leading if layer == 0 else jnp.logical_not(leading)
    piece = jnp.where(first, own[:, begin : begin + count], other[:, begin : begin + count])
    return piece.reshape(-1, piece.shape[-1])


def hand_over(lower, upper, leading):
    sent = jnp.where(leading, upper, lower)
    mine = jnp.where(leading, lower, upper)
    received = swapped(sent)
    return (jnp.where(leading, mine, received), jnp.where(leading, received, mine))


GAIN_ROWS = 16


def on_device(section_feeds, positions, w_qkv, w_out, w_gate_up, w_down, gains):
    leading = lax.axis_index("pipe") == 0
    pipe_rank = lax.axis_index("pipe")
    seq_rank = lax.axis_index("seq")
    seq_size = lax.axis_size("seq")
    owners = lax.axis_size("dp") * seq_size
    qkv_rows, out_rows = w_qkv.shape[2], w_out.shape[1]
    gate_up_rows, down_rows = w_gate_up.shape[2], w_down.shape[1]
    gain_count = gains.shape[1]
    gain_block = jnp.pad(gains, ((0, GAIN_ROWS - 1), (0, D - gain_count)))
    early = jnp.concatenate([w_qkv[0].T, w_out[0], gain_block], axis=0)
    late = jnp.concatenate([w_gate_up[0].T, w_down[0]], axis=0)
    early_chains = double(start_doubling(early), 2)
    late, early_chains = held_until(late, early_chains)
    early = doubled(early_chains)
    late_chains = start_doubling(late)

    def first_weights(layer):
        own_gains = rows_of(early, layer, leading, qkv_rows + out_rows, 1)
        return (
            rows_of(early, layer, leading, 0, qkv_rows),
            rows_of(early, layer, leading, qkv_rows, out_rows),
            own_gains[:, :gain_count].reshape(-1).astype(jnp.float32),
        )

    def late_pieces(pair, layer):
        return (
            rows_of(pair, layer, leading, 0, gate_up_rows),
            rows_of(pair, layer, leading, gate_up_rows, down_rows),
        )

    arrived = []

    class LowerLate:
        def begin(packed):
            return held_until(packed, double(late_chains, 2))

        def end(array, chains):
            own, other = doubled(chains)
            array, own, other = lax.optimization_barrier((array, own, other))
            arrived.append((own, other))
            return (array,) + late_pieces((own, other), 0)

    class UpperLate:
        def begin(packed):
            return (packed, None)

        def end(array, chains):
            return (array,) + late_pieces(arrived[0], 1)

    feeds = section_feeds[0, :, 0]
    micro_count, shard_rows = feeds.shape[:2]
    row_count = shard_rows // 2
    front, back = feeds[:, :row_count], feeds[:, row_count:]
    received = swapped(jnp.where(leading, back, front))
    first_in = jnp.where(leading, front, received).reshape(-1, D)
    last_grad = jnp.where(leading, received, back).reshape(-1, D)
    begin = pipe_rank * row_count
    position = lax.dynamic_slice_in_dim(positions[:, 0], begin, row_count, 1)
    local_rows = jnp.arange(row_count, dtype=jnp.int32)
    query_index = seq_rank * shard_rows + begin + local_rows
    key_index = (
        jnp.arange(2, dtype=jnp.int32)[:, None, None] * row_count
        + jnp.arange(seq_size, dtype=jnp.int32)[None, :, None] * shard_rows
        + local_rows[None, None, :]
    ).reshape(-1)
    query_index = jnp.tile(query_index, HEADS)
    query_place = jnp.tile(position, (1, HEADS))

    tables = (angle_tables(position, 1000000.0), angle_tables(position, 10000.0))
    visible = (
        visibility(query_index, query_place, key_index, None),
        visibility(query_index, query_place, key_index, WINDOW),
    )
    middle, kept_lower, lower = forward_layer(
        first_in.astype(jnp.float32), first_weights(0), tables[0], visible[0], LowerLate
    )
    middle = middle.astype(jnp.bfloat16).astype(jnp.float32)
    output, kept_upper, upper = forward_layer(
        middle, first_weights(1), tables[1], visible[1], UpperLate
    )
    output = output.astype(jnp.bfloat16)

    grad_middle, upper_chains, unused = backward_layer(
        last_grad.astype(jnp.float32), kept_upper, upper, tables[1], leading, []
    )
    grad_middle = grad_middle.astype(jnp.bfloat16).astype(jnp.float32)
    grad_input, lower_chains, upper_chains = backward_layer(
        grad_middle, kept_lower, lower, tables[0], leading, upper_chains
    )
    upper_parts = (finish(upper_chains[:2]), finish(upper_chains[2:]))
    lower_parts = (finish(lower_chains[:2]), finish(lower_chains[2:]))
    ends = hand_over(
        grad_input.astype(jnp.bfloat16).reshape(micro_count, row_count, D),
        output.reshape(micro_count, row_count, D),
        leading,
    )
    section_end = jnp.concatenate(ends, axis=1)
    late_grads = jnp.concatenate(hand_over(lower_parts[0], upper_parts[0], leading), axis=0)
    early_grads = jnp.concatenate(hand_over(lower_parts[1], upper_parts[1], leading), axis=0)
    late_grads = late_grads.astype(jnp.float32)
    early_grads = early_grads.astype(jnp.float32)
    return (
        section_end[None, :, None],
        early_grads[:qkv_rows].T[None],
        late_grads[gate_up_rows + down_rows :][None],
        late_grads[:gate_up_rows].T[None],
        late_grads[gate_up_rows : gate_up_rows + down_rows][None],
        early_grads[qkv_rows, :gain_count][None],
    )


def solution(mesh):
    in_specs = (
        P("pipe", None, "dp", "seq", None),
        P(None, "dp", "seq"),
        P("pipe", None, ("dp", "seq")),
        P("pipe", ("dp", "seq"), None),
        P("pipe", None, ("dp", "seq")),
        P("pipe", ("dp", "seq"), None),
        P("pipe", ("dp", "seq")),
    )
    out_specs = (
        P("pipe", None, "dp", "seq", None),
        P("pipe", None, ("dp", "seq")),
        P("pipe", ("dp", "seq"), None),
        P("pipe", None, ("dp", "seq")),
        P("pipe", ("dp", "seq"), None),
        P("pipe", ("dp", "seq")),
    )
    return jax.shard_map(
        on_device, mesh=mesh, in_specs=in_specs, out_specs=out_specs, check_vma=False
    )
```
